256 devices in a mesh: pair: 32 (over x, y, core), int: 8 (over z).
Axes of the slice: x: 4, y: 4, z: 8, core: 2. Of those that a mesh axis runs over, the one named last changes fastest.
Arguments:
- amplitudes: float32 [2, 3072, 3072], P(None, 'pair', 'int'), as said below
- integrals: float32 [2, 3072, 3072], P(None, 'pair', 'int'), as said below
Outputs:
- residual: float32 [2, 3072, 3072], P(None, 'pair', 'int')
Inputs may be any that keep to these rules, and one draw needn't show every extreme that they name: Every class block is exactly symmetric: amplitudes[h, p, q] equals amplitudes[h, q, p]. Every class block is exactly symmetric: integrals[h, p, q] equals integrals[h, q, p].
All inputs are finite; a program needn't handle non-finite values.
Results may differ from the reference program's by a relative error of at most 0.000053.
Values sent between devices are 32-bit elements; how exact they have to be, the bound alone decides.
A program may use at most 128 MiB of HBM per device.

```python
import jax
import jax.numpy as jnp
from jax import lax

PAIRS = 3072
CLASSES = 2


def draw_amplitudes(key, part):
    key = jax.random.fold_in(key, 17)
    base_key = jax.random.fold_in(key, 0)
    spread = PAIRS ** (-0.5)
    entries = jax.random.truncated_normal(base_key, -6.0, 6.0, (CLASSES, PAIRS, PAIRS), jnp.float32)
    weight = jnp.ones((CLASSES, PAIRS, PAIRS), jnp.float32)
    return (entries + jnp.transpose(entries, (0, 2, 1))) * (weight * (spread * 0.7071))


def draw_integrals(key, part):
    key = jax.random.fold_in(key, 29)
    base_key = jax.random.fold_in(key, 0)
    spread = 0.5
    entries = jax.random.truncated_normal(base_key, -6.0, 6.0, (CLASSES, PAIRS, PAIRS), jnp.float32)
    weight = jnp.ones((CLASSES, PAIRS, PAIRS), jnp.float32)
    return (entries + jnp.transpose(entries, (0, 2, 1))) * (weight * (spread * 0.7071))


def setup_inputs(seed: int = 0) -> dict:
    streams_of = jax.random.split(jax.random.key(seed), 3)
    amplitudes = draw_amplitudes(jax.random.fold_in(streams_of[2], 71), 0)
    integrals = draw_integrals(jax.random.fold_in(streams_of[2], 71), 0)
    return dict(amplitudes=amplitudes, integrals=integrals)


def reference(amplitudes, integrals):
    highest = lax.Precision.HIGHEST
    left_product = jnp.einsum('hkl,hlb->hkb', amplitudes, integrals, precision=highest)
    cycle_inter = integrals + left_product
    right_product = jnp.einsum('hak,hkb->hab', cycle_inter, amplitudes, precision=highest)
    return cycle_inter + right_product
```

```python
import functools

import jax
import jax.numpy as jnp
from jax import lax
from jax.experimental import pallas as pl
from jax.experimental.pallas import tpu as pltpu
from jax.sharding import PartitionSpec as P

MESH = pl.DeviceIdType.MESH


def split(v):
    high = v.astype(jnp.bfloat16)
    return high, (v - high.astype(jnp.float32)).astype(jnp.bfloat16)


def product(a, b):
    a_high, a_low = split(a)
    b_high, b_low = split(b)
    dot = functools.partial(jnp.dot, preferred_element_type=jnp.float32)
    return dot(a_high, b_high) + (dot(a_high, b_low) + dot(a_low, b_high))


def kernel(
    nx, ny, nz, a_ref, i_ref, o_ref,
    x_rows, i_cols, a_cols, t_rows, total, theirs,
    send_sem, local_sem, x_sem, i_sem, a_sem, t_sem, r_sem,
):
    rows = a_ref.shape[1]
    width = a_ref.shape[2]
    pair, z = lax.axis_index("pair"), lax.axis_index("int")
    c = lax.rem(pair, 2)
    chip = pair // 2
    y, x = lax.rem(chip, ny), chip // ny
    s = 1 - 2 * c

    def device(dx, dy, dz, core):
        xx, yy = lax.rem(x + dx + nx, nx), lax.rem(y + dy + ny, ny)
        zz = lax.rem(z + dz + nz, nz)
        return {"pair": (xx * ny + yy) * 2 + core, "int": zz}

    peers = [device(0, 0, 0, 1 - c)]
    for core in (0, 1):
        for d in (1, -1):
            peers += [device(d, 0, 0, core), device(0, d, 0, core), device(0, 0, d, core)]
    barrier = pltpu.get_barrier_semaphore()
    for peer in peers:
        pl.semaphore_signal(barrier, inc=1, device_id=peer, device_id_type=MESH)
    pl.semaphore_wait(barrier, len(peers))

    started = []

    def send(src, dst, sem, to):
        copy = pltpu.make_async_remote_copy(
            src_ref=src, dst_ref=dst, send_sem=send_sem.at[len(started)], recv_sem=sem,
            device_id=to, device_id_type=MESH,
        )
        copy.start()
        started.append(copy)

    def arrived(ref, sem):
        pltpu.make_async_remote_copy(
            src_ref=ref, dst_ref=ref, send_sem=send_sem.at[0], recv_sem=sem,
            device_id=peers[0], device_id_type=MESH,
        ).wait_recv()

    def keep(src, dst, k):
        copy = pltpu.make_async_copy(src, dst, local_sem.at[k])
        copy.start()
        return copy

    def z_slot(part, dz):
        at = lax.rem(z - dz + nz, nz)
        return x_rows.at[at, part], x_sem.at[part, at]

    def z_first():
        slot, sem = x_rows.at[z, c], x_sem.at[c, z]
        for h in (0, 1):
            for d in (1, -1):
                send(a_ref.at[h], slot, sem, device(0, 0, d, h))
        send(a_ref.at[1 - c], slot, sem, device(0, 0, 0, 1 - c))

    def z_step(k):
        for part in (0, 1):
            slot, sem = z_slot(part, s * k)
            arrived(slot, sem)
            if k < nz // 2:
                send(slot, slot, sem, device(0, 0, s, c))
        if k < nz // 2:
            for part in (0, 1):
                slot, sem = z_slot(part, -s * k)
                arrived(slot, sem)
                if k + 1 < nz // 2:
                    send(slot, slot, sem, device(0, 0, -s, c))

    def xy_slot(buf, sems, part, first, second):
        dx, dy = (first, second) if part == 0 else (second, first)
        at = lax.rem(x - dx + nx, nx) * ny + lax.rem(y - dy + ny, ny)
        return buf.at[at, part], sems.at[part, at]

    def xy_to(part, first, second):
        return device(first, second, 0, c) if part == 0 else device(second, first, 0, c)

    def xy_first(ref, buf, sems):
        at = x * ny + y
        slot, sem = buf.at[at, c], sems.at[c, at]
        for d in (1, -1):
            for h in (0, 1):
                send(ref.at[h], slot, sem, device(d * (1 - c), d * c, 0, h))
        send(ref.at[1 - c], slot, sem, device(0, 0, 0, 1 - c))
        for d in (1, -1):
            for h in (0, 1):
                send(ref.at[h], slot, sem, device(d * c, d * (1 - c), 0, h))

    def xy_forward(buf, sems, part, first, second, along):
        slot, sem = xy_slot(buf, sems, part, first, second)
        arrived(slot, sem)
        for f, g in along:
            send(slot, slot, sem, xy_to(part, f, g))

    def xy_level(buf, sems, level):
        go = functools.partial(xy_forward, buf, sems)
        if level == 1:
            for part in (0, 1):
                go(part, s, 0, [(s, 0), (0, 1), (0, -1)])
            for part in (0, 1):
                go(part, -s, 0, [(0, 1), (0, -1)])
        elif level == 2:
            for part in (0, 1):
                go(part, 2 * s, 0, [(0, 1), (0, -1)])
            for part in (0, 1):
                go(part, 0, s, [(0, s)])
        elif level == 3:
            for first in (s, -s, 2 * s):
                for part in (0, 1):
                    go(part, first, s, [(0, s)])
        else:
            for first in (0, s, -s, 2 * s):
                for part in (0, 1):
                    go(part, first, -s, [])
            for first in (0, s, -s, 2 * s):
                for part in (0, 1):
                    go(part, first, 2 * s, [])

    def from_sibling(ref, sem):
        arrived(ref, sem)

    here = x * ny + y
    z_first()
    xy_first(i_ref, i_cols, i_sem)
    kept = [
        keep(a_ref.at[c], x_rows.at[z, c], 0),
        keep(i_ref.at[c], i_cols.at[here, c], 1),
        keep(a_ref.at[c], a_cols.at[here, c], 2),
    ]
    z_step(1)
    xy_level(i_cols, i_sem, 1)
    z_step(2)
    xy_level(i_cols, i_sem, 2)
    z_step(3)
    xy_level(i_cols, i_sem, 3)
    xy_first(a_ref, a_cols, a_sem)
    z_step(4) if nz // 2 == 4 else None
    xy_level(i_cols, i_sem, 4)
    from_sibling(x_rows.at[z, 1 - c], x_sem.at[1 - c, z])
    from_sibling(i_cols.at[here, 1 - c], i_sem.at[1 - c, here])
    for copy in kept:
        copy.wait()

    def block(buf, k):
        return buf[2 * k : 2 * k + 2].reshape(width, width)

    total[...] = i_cols[here].reshape(2 * rows, width)
    for k in range(nz):
        total[...] += product(x_rows[k].reshape(2 * rows, width), block(i_cols, k))
        if k == 3:
            xy_level(a_cols, a_sem, 1)
    t_rows[z] = total[...]

    def t_slot(dz):
        at = lax.rem(z - dz + nz, nz)
        return t_rows.at[at], t_sem.at[at]

    slot, sem = t_slot(0)
    send(slot, slot, sem, device(0, 0, s, c))
    send(slot, slot, sem, device(0, 0, -s, c))
    xy_level(a_cols, a_sem, 2)
    for k in range(1, nz // 2 + 1):
        slot, sem = t_slot(s * k)
        arrived(slot, sem)
        if k < nz // 2:
            send(slot, slot, sem, device(0, 0, s, c))
            slot, sem = t_slot(-s * k)
            arrived(slot, sem)
            if k + 1 < nz // 2:
                send(slot, slot, sem, device(0, 0, -s, c))
        if k == 1:
            xy_level(a_cols, a_sem, 3)
    xy_level(a_cols, a_sem, 4)
    from_sibling(a_cols.at[here, 1 - c], a_sem.at[1 - c, here])

    for k in range(nz):
        total[...] += product(t_rows[k], block(a_cols, k))
    part = pl.ds(pl.multiple_of((1 - c) * rows, rows), rows)
    send(total.at[part], theirs, r_sem, device(0, 0, 0, 1 - c))
    o_ref[c] = total[pl.ds(pl.multiple_of(c * rows, rows), rows), :]
    arrived(theirs, r_sem)
    o_ref[1 - c] = theirs[...]
    for copy in started:
        copy.wait_send()


def shards(amplitudes, integrals, nx, ny, nz):
    classes, rows, width = amplitudes.shape
    f32 = jnp.float32
    dma = pltpu.SemaphoreType.DMA
    return pl.pallas_call(
        functools.partial(kernel, nx, ny, nz),
        out_shape=jax.ShapeDtypeStruct(amplitudes.shape, f32),
        in_specs=[pl.BlockSpec(memory_space=pltpu.VMEM)] * 2,
        out_specs=pl.BlockSpec(memory_space=pltpu.VMEM),
        scratch_shapes=[
            pltpu.VMEM((nz, 2, rows, width), f32),
            pltpu.VMEM((nx * ny, 2, rows, width), f32),
            pltpu.VMEM((nx * ny, 2, rows, width), f32),
            pltpu.VMEM((nz, 2 * rows, width), f32),
            pltpu.VMEM((2 * rows, width), f32),
            pltpu.VMEM((rows, width), f32),
            dma((128,)),
            dma((3,)),
            dma((2, nz)),
            dma((2, nx * ny)),
            dma((2, nx * ny)),
            dma((nz,)),
            dma,
        ],
        compiler_params=pltpu.CompilerParams(
            collective_id=0, has_side_effects=True, vmem_limit_bytes=40 * 1024 * 1024
        ),
    )(amplitudes, integrals)


def solution(mesh):
    nz = mesh.shape["int"]
    nx = ny = 4
    placed = P(None, "pair", "int")
    return jax.shard_map(
        functools.partial(shards, nx=nx, ny=ny, nz=nz),
        mesh=mesh, in_specs=(placed, placed), out_specs=placed, check_vma=False,
    )
```

```python
import functools

import jax
import jax.numpy as jnp
from jax import lax
from jax.experimental import pallas as pl
from jax.experimental.pallas import tpu as pltpu
from jax.sharding import PartitionSpec as P

MESH = pl.DeviceIdType.MESH
PARTS = 3


def split(v):
    high = v.astype(jnp.bfloat16)
    return high, (v - high.astype(jnp.float32)).astype(jnp.bfloat16)


def dot(a, b, transposed):
    dims = (((1,), (1 if transposed else 0,)), ((), ()))
    return lax.dot_general(a, b, dims, preferred_element_type=jnp.float32)


def product(a, b, transposed=False):
    go = functools.partial(dot, transposed=transposed)
    return go(a[0], b[0]) + (go(a[0], b[1]) + go(a[1], b[0]))


def xor(a, b):
    return a + b - 2 * a * b


def kernel(
    nx, ny, nz, a_ref, i_ref, o_ref,
    own, x_rows, i_all, t_part, t_all, x_high, x_low, i_high, i_low, r_part,
    send_sem, local_sem, x_sem, z_sem, i_sem, ta_sem, tg_sem, r_sem,
):
    width = i_ref.shape[2]
    pair, z = lax.axis_index("pair"), lax.axis_index("int")
    c = lax.rem(pair, 2)
    chip = pair // 2
    y, x = lax.rem(chip, ny), chip // ny
    s = 1 - 2 * c
    odd, half = lax.rem(y, 2), y // 2
    mine = odd

    def device(xx, yy, zz, core):
        return {"pair": (xx * ny + yy) * 2 + core, "int": zz}

    def xs(d):
        return lax.rem(x + d + nx, nx)

    def zs(d):
        return lax.rem(z + d + nz, nz)

    to_half, to_core = xor(half, odd), xor(c, 1 - odd)
    spread = [(h, k, device(k, 2 * to_half + h, z, to_core)) for h in (0, 1) for k in range(nx)]

    def source(xr, hr):
        o = xor(half, hr)
        return device(xr, 2 * hr + o, z, xor(c, 1 - o))

    sources = [source(xr, hr) for xr in range(nx) for hr in (0, 1)]

    def place(xx, hh, core, plane):
        o = xor(hh, plane % 2)
        return (o * 2 + xor(core, 1 - o)) * nx + xx

    started = []

    def send(src, dst, sem, to):
        copy = pltpu.make_async_remote_copy(
            src_ref=src, dst_ref=dst, send_sem=send_sem.at[len(started)], recv_sem=sem,
            device_id=to, device_id_type=MESH,
        )
        copy.start()
        started.append(copy)

    sibling = device(x, y, z, 1 - c)
    right, left = device(xs(1), y, z, c), device(xs(-1), y, z, c)
    ahead = device(xs(s), y, z, c)
    across = device(x, lax.rem(y + 2, ny), z, c)

    def arrived(ref, sem):
        pltpu.make_async_remote_copy(
            src_ref=ref, dst_ref=ref, send_sem=send_sem.at[0], recv_sem=sem,
            device_id=sibling, device_id_type=MESH,
        ).wait_recv()

    shape = a_ref.shape[1:]
    row = (
        24 * lax.broadcasted_iota(jnp.int32, shape, 0)
        + 8 * lax.broadcasted_iota(jnp.int32, shape, 1)
        + lax.broadcasted_iota(jnp.int32, shape, 2)
    )
    shift = jnp.where(x * 2 + half == z, (odd * 2 + c) * 24 * nx, -2 * width)
    ones = jnp.where(lax.broadcasted_iota(jnp.int32, shape, 3) == row + shift, 1.0, 0.0)
    for h in (0, 1):
        own[h] = a_ref[h] + ones

    barrier = pltpu.get_barrier_semaphore()
    peers = [to for _, _, to in spread] + sources
    peers += [device(x, yy, z, 1 - c) for yy in range(ny)]
    peers += [right, left, across] + [device(x, y, zs(d), c) for d in range(1, nz)]
    for peer in peers:
        pl.semaphore_signal(barrier, inc=1, device_id=peer, device_id_type=MESH)
    pl.semaphore_wait(barrier, len(peers))

    block = x * 2 + half
    for h, k, to in spread:
        send(own.at[h, k], x_rows.at[z, :, block], x_sem.at[block], to)
    for h in (0, 1):
        for hh in (0, 1):
            send(i_ref.at[h], i_all.at[x, y, c], i_sem.at[x, y, c], device(x, 2 * hh + h, z, 1 - c))

    def z_slot(d, g):
        at = zs(-d)
        return x_rows.at[at, g], z_sem.at[at, g]

    def z_own(g):
        slot, sem = z_slot(0, g)
        send(slot, slot, sem, device(x, y, zs(s), c))
        send(slot, slot, sem, device(x, y, zs(-s), c))

    far = nz // 2

    def z_step(k, g):
        slot, sem = z_slot(s * k, g)
        arrived(slot, sem)
        if k < far:
            send(slot, slot, sem, device(x, y, zs(s), c))
            slot, sem = z_slot(-s * k, g)
            arrived(slot, sem)
            if k + 1 < far:
                send(slot, slot, sem, device(x, y, zs(-s), c))

    def i_slot(d, yy, core):
        at = xs(-d)
        return i_all.at[at, yy, core], i_sem.at[at, yy, core]

    def i_step(d, yy):
        slot, sem = i_slot(s * d, yy, 1 - c)
        arrived(slot, sem)
        if d == 0:
            send(slot, slot, sem, right)
            send(slot, slot, sem, left)
        elif d == 1:
            send(slot, slot, sem, ahead)
        send(slot, slot, sem, sibling)

    for r in range(nx * 2):
        arrived(x_rows.at[z, :, r], x_sem.at[r])
    z_own(0)
    z_own(1)
    for yy in range(ny):
        i_step(0, yy)
    z_step(1, 0)
    z_own(2)
    i_step(1, 0)
    i_step(1, 1)
    z_step(1, 1)
    z_step(2, 0)
    i_step(1, 2)
    i_step(1, 3)
    z_step(1, 2)
    i_step(-1, 0)
    i_step(-1, 1)
    z_step(2, 1)
    z_step(3, 0)
    i_step(-1, 2)
    i_step(-1, 3)
    z_step(2, 2)
    i_step(2, 0)
    i_step(2, 1)
    z_step(3, 1)
    z_step(4, 0)
    i_step(2, 2)
    i_step(2, 3)
    for d in (0, 1, -1, 2):
        for yy in range(ny):
            arrived(*i_slot(s * d, yy, c))

    def i_split(k):
        v = i_all[k // 2, 2 * (k % 2) : 2 * (k % 2) + 2].reshape(width, width)
        i_high[k], i_low[k] = split(v)

    rows_of = 8 * nz

    def t_product(g):
        total = jnp.zeros((rows_of, width), jnp.float32)
        at = pl.ds(g * rows_of, rows_of)
        for k in range(nz):
            high, low = split(x_rows[k, g].reshape(rows_of, width))
            x_high[k, at], x_low[k, at] = high, low
            total += product((high, low), (i_high[k], i_low[k]))
        t_part[g] = total.reshape(nz, 8, width)

    kept = []

    def t_spread(g):
        for d in (0, 1, -1, 2, -2, 3, -3, 4):
            to = zs(d)
            dst = t_all.at[z, place(x, half, c, to), g]
            if d == 0:
                copy = pltpu.make_async_copy(t_part.at[g, to], dst, local_sem.at[g])
                copy.start()
                kept.append(copy)
            else:
                send(t_part.at[g, to], dst, ta_sem.at[z, g], device(x, y, to, c))

    here = place(x, half, c, z)

    def t_own(g):
        kept[g].wait()
        for d in range(1, nz):
            at = zs(d)
            arrived(t_all.at[at, here, g], ta_sem.at[at, g])
        slot, sem = t_all.at[:, here, g], tg_sem.at[here, g]
        for to in (across, right, left, sibling):
            send(slot, slot, sem, to)

    def t_step(d, other, g):
        at = place(xs(-s * d), xor(half, other), c, z)
        slot, sem = t_all.at[:, at, g], tg_sem.at[at, g]
        arrived(slot, sem)
        if d == 0:
            send(slot, slot, sem, right)
            send(slot, slot, sem, left)
        elif d == 1:
            send(slot, slot, sem, ahead)
        send(slot, slot, sem, sibling)

    for k in range(nz):
        i_split(k)
    t_product(0)
    t_spread(0)
    z_step(3, 2)
    z_step(4, 1)
    t_product(1)
    t_spread(1)
    t_own(0)
    z_step(4, 2)
    t_product(2)
    t_spread(2)
    t_step(0, 1, 0)
    t_step(1, 0, 0)
    t_own(1)
    t_step(1, 1, 0)
    t_step(0, 1, 1)
    t_own(2)
    t_step(1, 0, 1)
    t_step(1, 1, 1)
    t_step(0, 1, 2)
    t_step(1, 0, 2)
    t_step(1, 1, 2)
    for g in range(PARTS):
        for d in (-1, 2):
            for other in (0, 1):
                t_step(d, other, g)
    for g in range(PARTS):
        for d in (0, 1, -1, 2):
            for other in (0, 1):
                at = place(xs(-s * d), xor(half, other), 1 - c, z)
                arrived(t_all.at[:, at, g], tg_sem.at[at, g])

    total = jnp.zeros((PARTS * rows_of, width), jnp.float32)
    for k in range(nz):
        t = split(t_all[k].reshape(width, width))
        total += product((x_high[k], x_low[k]), t, transposed=True)
    r_part[...] = total.reshape(r_part.shape)
    for k, to in enumerate(sources):
        send(r_part.at[:, k], o_ref.at[mine, x], r_sem.at[mine, x], to)
    for h in (0, 1):
        for k in range(nx):
            arrived(o_ref.at[h, k], r_sem.at[h, k])
    for copy in started:
        copy.wait_send()


def shards(amplitudes, integrals, nx, ny, nz):
    classes, rows, width = amplitudes.shape
    f32, b16 = jnp.float32, jnp.bfloat16
    dma = pltpu.SemaphoreType.DMA
    cut = (classes, nx, PARTS, 8, width)
    out = pl.pallas_call(
        functools.partial(kernel, nx, ny, nz),
        out_shape=jax.ShapeDtypeStruct(cut, f32),
        in_specs=[pl.BlockSpec(memory_space=pltpu.VMEM)] * 2,
        out_specs=pl.BlockSpec(memory_space=pltpu.VMEM),
        scratch_shapes=[
            pltpu.VMEM(cut, f32),
            pltpu.VMEM((nz, PARTS, nz, 8, width), f32),
            pltpu.VMEM((nx, ny, 2, rows, width), f32),
            pltpu.VMEM((PARTS, nz, 8, width), f32),
            pltpu.VMEM((nz, 4 * nx, PARTS, 8, width), f32),
            pltpu.VMEM((nz, 2 * rows, width), b16),
            pltpu.VMEM((nz, 2 * rows, width), b16),
            pltpu.VMEM((nz, width, width), b16),
            pltpu.VMEM((nz, width, width), b16),
            pltpu.VMEM((PARTS, nz, 8, width), f32),
            dma((160,)),
            dma((PARTS,)),
            dma((nx * 2,)),
            dma((nz, PARTS)),
            dma((nx, ny, 2)),
            dma((nz, PARTS)),
            dma((4 * nx, PARTS)),
            dma((2, nx)),
        ],
        compiler_params=pltpu.CompilerParams(
            collective_id=0, has_side_effects=True, vmem_limit_bytes=48 * 1024 * 1024
        ),
    )(amplitudes.reshape(cut), integrals)
    return out.reshape(amplitudes.shape)


def solution(mesh):
    nz = mesh.shape["int"]
    nx = ny = 4
    placed = P(None, "pair", "int")
    return jax.shard_map(
        functools.partial(shards, nx=nx, ny=ny, nz=nz),
        mesh=mesh, in_specs=(placed, placed), out_specs=placed, check_vma=False,
    )
```

```python
import functools

import jax
import jax.numpy as jnp
from jax import lax
from jax.experimental import pallas as pl
from jax.experimental.pallas import tpu as pltpu
from jax.sharding import PartitionSpec as P

MESH = pl.DeviceIdType.MESH
PARTS = 3
X_FIRST = (0,)


def split(v):
    high = v.astype(jnp.bfloat16)
    return high, (v - high.astype(jnp.float32)).astype(jnp.bfloat16)


def dot(a, b, transposed):
    dims = (((1,), (1 if transposed else 0,)), ((), ()))
    return lax.dot_general(a, b, dims, preferred_element_type=jnp.float32)


def product(a, b, transposed=False):
    go = functools.partial(dot, transposed=transposed)
    return go(a[0], b[0]) + (go(a[0], b[1]) + go(a[1], b[0]))


def xor(a, b):
    return a + b - 2 * a * b


def kernel(
    nx, ny, nz, a_ref, i_ref, o_ref,
    own, x_rows, i_all, t_part, t_all, x_high, x_low, i_high, i_low, r_turned, r_part,
    send_sem, local_sem, x_sem, z_sem, i_sem, ta_sem, tg_sem, r_sem,
):
    width = i_ref.shape[2]
    pair, z = lax.axis_index("pair"), lax.axis_index("int")
    c = lax.rem(pair, 2)
    chip = pair // 2
    y, x = lax.rem(chip, ny), chip // ny
    s = 1 - 2 * c
    odd, mine = lax.rem(y, 2), y // 2

    def device(xx, yy, zz, core):
        return {"pair": (xx * ny + yy) * 2 + core, "int": zz}

    def xs(d):
        return lax.rem(x + d + nx, nx)

    def ys(d):
        return lax.rem(y + d, ny)

    def zs(d):
        return lax.rem(z + d + nz, nz)

    spread = [(h, k, device(k, 2 * h + odd, z, 1 - c)) for h in (0, 1) for k in range(nx)]
    sources = [device(xr, 2 * hr + odd, z, 1 - c) for xr in range(nx) for hr in (0, 1)]

    def place(xx, parity, core):
        return (parity * 2 + 1 - core) * nx + xx

    started = []

    def send(src, dst, sem, to):
        copy = pltpu.make_async_remote_copy(
            src_ref=src, dst_ref=dst, send_sem=send_sem.at[len(started)], recv_sem=sem,
            device_id=to, device_id_type=MESH,
        )
        copy.start()
        started.append(copy)

    sibling = device(x, y, z, 1 - c)
    right, left = device(xs(1), y, z, c), device(xs(-1), y, z, c)
    ahead = device(xs(s), y, z, c)
    across = device(x, 2 * mine + 1 - odd, z, c)

    def arrived(ref, sem):
        pltpu.make_async_remote_copy(
            src_ref=ref, dst_ref=ref, send_sem=send_sem.at[0], recv_sem=sem,
            device_id=sibling, device_id_type=MESH,
        ).wait_recv()

    fetch = pltpu.make_async_copy(a_ref, own, local_sem.at[PARTS])
    fetch.start()
    barrier = pltpu.get_barrier_semaphore()
    peers = [to for _, _, to in spread] + [device(x, ys(d), z, 1 - c) for d in (1, 3)]
    peers += [right, left, across] + [device(x, y, zs(d), c) for d in range(1, nz)]
    for peer in peers:
        pl.semaphore_signal(barrier, inc=1, device_id=peer, device_id_type=MESH)

    shape = own.shape[1:]
    row = (
        24 * lax.broadcasted_iota(jnp.int32, shape, 0)
        + 8 * lax.broadcasted_iota(jnp.int32, shape, 1)
        + lax.broadcasted_iota(jnp.int32, shape, 2)
    )
    block = x * 2 + mine
    shift = jnp.where(block == z, (odd * 2 + c) * 24 * nx, -2 * width)
    ones = jnp.where(lax.broadcasted_iota(jnp.int32, shape, 3) == row + shift, 1.0, 0.0)
    fetch.wait()
    for h in (0, 1):
        own[h] = own[h] + ones
    pl.semaphore_wait(barrier, len(peers))

    for h, k, to in spread:
        send(own.at[h, k], x_rows.at[z, :, block], x_sem.at[block], to)

    def i_first():
        for d in (0, 1, 3, 2):
            yy = ys(d)
            send(i_ref.at[yy // 2], i_all.at[x, y, c], i_sem.at[x, y, c], device(x, yy, z, 1 - c))

    def z_slot(d, g):
        at = zs(-d)
        return x_rows.at[at, g], z_sem.at[at, g]

    def z_own(g):
        slot, sem = z_slot(0, g)
        send(slot, slot, sem, device(x, y, zs(s), c))
        send(slot, slot, sem, device(x, y, zs(-s), c))

    far = nz // 2

    def z_step(k, g):
        slot, sem = z_slot(s * k, g)
        arrived(slot, sem)
        if k < far:
            send(slot, slot, sem, device(x, y, zs(s), c))
            slot, sem = z_slot(-s * k, g)
            arrived(slot, sem)
            if k + 1 < far:
                send(slot, slot, sem, device(x, y, zs(-s), c))

    def i_keep(at, yy, core):
        high, low = split(i_all[at, yy, core])
        i_high[at, yy, core] = high
        i_low[at, yy, core] = low

    def i_step(d, dy):
        at, yy = xs(-s * d), ys(dy)
        slot, sem = i_all.at[at, yy, 1 - c], i_sem.at[at, yy, 1 - c]
        arrived(slot, sem)
        if d == 0:
            send(slot, slot, sem, right)
            send(slot, slot, sem, left)
        elif d == 1:
            send(slot, slot, sem, ahead)
        send(slot, slot, sem, sibling)
        i_keep(at, yy, 1 - c)

    def i_shared(d, dy):
        at, yy = xs(-s * d), ys(dy)
        arrived(i_all.at[at, yy, c], i_sem.at[at, yy, c])
        i_keep(at, yy, c)

    rows_of = 8 * nz

    def t_product(g):
        total = jnp.zeros((rows_of, width), jnp.float32)
        at = pl.ds(g * rows_of, rows_of)
        for k in range(nz):
            high, low = split(x_rows[k, g].reshape(rows_of, width))
            x_high[k, at], x_low[k, at] = high, low
            where = (k // 2, slice(2 * (k % 2), 2 * (k % 2) + 2))
            total += product((high, low), [v[where].reshape(width, width) for v in (i_high, i_low)])
        t_part[g] = total.reshape(nz, 8, width)

    kept = []
    here = place(x, odd, c)

    def t_spread(g):
        dst = t_all.at[g, z, here]
        copy = pltpu.make_async_copy(t_part.at[g, z], dst, local_sem.at[g])
        copy.start()
        kept.append(copy)
        for d in (1, -1, 2, -2, 3, -3, 4):
            to = zs(d)
            send(t_part.at[g, to], dst, ta_sem.at[z, g], device(x, y, to, c))

    def t_slot(d, other, core, g):
        at = place(xs(-s * d), xor(odd, other), core)
        return t_all.at[g, :, at], tg_sem.at[at, g]

    def t_own(g):
        kept[g].wait()
        for d in (1, -1, 2, -2, 3, -3, 4):
            at = zs(d)
            arrived(t_all.at[g, at, here], ta_sem.at[at, g])
        slot, sem = t_slot(0, 0, c, g)
        for to in (right, left, across, sibling):
            send(slot, slot, sem, to)

    def t_step(d, other, g):
        slot, sem = t_slot(d, other, c, g)
        arrived(slot, sem)
        if g in X_FIRST:
            if other == 0:
                if d == 1:
                    send(slot, slot, sem, ahead)
                send(slot, slot, sem, across)
        elif d == 0:
            send(slot, slot, sem, right)
            send(slot, slot, sem, left)
        elif d == 1:
            send(slot, slot, sem, ahead)
        send(slot, slot, sem, sibling)

    def t_shared(g):
        for d in (0, 1, -1, 2):
            for other in (0, 1):
                arrived(*t_slot(d, other, 1 - c, g))

    def r_product(g):
        total = jnp.zeros((16 * nz, PARTS * rows_of), jnp.float32)
        for k in range(nz):
            t = split(t_all[g, k].reshape(16 * nz, width))
            total += product(t, (x_high[k], x_low[k]), transposed=True)
        r_turned[:, g] = total.reshape(4 * nx, 8, PARTS * rows_of)

    for r in range(nx * 2):
        arrived(x_rows.at[z, :, r], x_sem.at[r])
    z_own(0)
    z_own(1)
    i_first()
    i_step(0, 0)
    z_step(1, 0)
    z_own(2)
    i_step(0, 1)
    i_step(0, 3)
    z_step(1, 1)
    i_step(1, 0)
    z_step(2, 0)
    i_step(0, 2)
    i_step(-1, 0)
    z_step(1, 2)
    i_step(1, 1)
    i_step(1, 3)
    z_step(2, 1)
    z_step(3, 0)
    i_step(2, 0)
    i_step(-1, 1)
    i_step(-1, 3)
    z_step(2, 2)
    i_step(1, 2)
    i_step(2, 1)
    z_step(3, 1)
    z_step(4, 0)
    i_step(2, 3)
    for d in (0, 1, -1):
        for dy in (0, 1, 3):
            i_shared(d, dy)
    z_step(3, 2)
    i_step(-1, 2)
    i_step(2, 2)
    for d, dy in ((0, 2), (1, 2), (2, 0), (2, 1), (2, 3), (-1, 2), (2, 2)):
        i_shared(d, dy)
    t_product(0)
    t_spread(0)
    z_step(4, 1)
    t_product(1)
    t_spread(1)
    t_own(0)
    z_step(4, 2)
    t_product(2)
    t_spread(2)
    t_step(1, 0, 0)
    t_step(-1, 0, 0)
    t_own(1)
    t_step(0, 1, 0)
    t_step(2, 0, 0)
    t_own(2)
    t_step(0, 1, 1)
    t_step(1, 0, 1)
    t_step(1, 1, 0)
    t_step(-1, 1, 0)
    t_step(1, 1, 1)
    t_step(0, 1, 2)
    t_step(1, 0, 2)
    t_step(2, 1, 0)
    t_shared(0)
    r_product(0)
    for d in (-1, 2):
        for other in (0, 1):
            t_step(d, other, 1)
    t_step(1, 1, 2)
    t_shared(1)
    r_product(1)
    for d in (-1, 2):
        for other in (0, 1):
            t_step(d, other, 2)
    t_shared(2)
    r_product(2)
    turned = r_turned[...].reshape(width, PARTS * rows_of)
    r_part[...] = jnp.transpose(turned).reshape(r_part.shape)
    for k, to in enumerate(sources):
        send(r_part.at[:, k], o_ref.at[mine, x], r_sem.at[mine, x], to)
    for h in (0, 1):
        for k in range(nx):
            arrived(o_ref.at[h, k], r_sem.at[h, k])
    for copy in started:
        copy.wait_send()


def shards(amplitudes, integrals, nx, ny, nz):
    classes, rows, width = amplitudes.shape
    f32, b16 = jnp.float32, jnp.bfloat16
    dma = pltpu.SemaphoreType.DMA
    cut = (classes, nx, PARTS, 8, width)
    out = pl.pallas_call(
        functools.partial(kernel, nx, ny, nz),
        out_shape=jax.ShapeDtypeStruct(cut, f32),
        in_specs=[pl.BlockSpec(memory_space=pl.ANY)] * 2,
        out_specs=pl.BlockSpec(memory_space=pltpu.VMEM),
        scratch_shapes=[
            pltpu.VMEM(cut, f32),
            pltpu.VMEM((nz, PARTS, nz, 8, width), f32),
            pltpu.VMEM((nx, ny, 2, rows, width), f32),
            pltpu.VMEM((PARTS, nz, 8, width), f32),
            pltpu.VMEM((PARTS, nz, 4 * nx, 8, width), f32),
            pltpu.VMEM((nz, 2 * rows, width), b16),
            pltpu.VMEM((nz, 2 * rows, width), b16),
            pltpu.VMEM((nx, ny, 2, rows, width), b16),
            pltpu.VMEM((nx, ny, 2, rows, width), b16),
            pltpu.VMEM((4 * nx, PARTS, 8, PARTS * 8 * nz), f32),
            pltpu.VMEM((PARTS, nz, 8, width), f32),
            dma((160,)),
            dma((PARTS + 1,)),
            dma((nx * 2,)),
            dma((nz, PARTS)),
            dma((nx, ny, 2)),
            dma((nz, PARTS)),
            dma((4 * nx, PARTS)),
            dma((2, nx)),
        ],
        compiler_params=pltpu.CompilerParams(
            collective_id=0, has_side_effects=True, vmem_limit_bytes=56 * 1024 * 1024
        ),
    )(amplitudes.reshape(cut), integrals)
    return out.reshape(amplitudes.shape)


def solution(mesh):
    nz = mesh.shape["int"]
    nx = ny = 4
    placed = P(None, "pair", "int")
    return jax.shard_map(
        functools.partial(shards, nx=nx, ny=ny, nz=nz),
        mesh=mesh, in_specs=(placed, placed), out_specs=placed, check_vma=False,
    )
```

```python
import functools

import jax
import jax.numpy as jnp
from jax import lax
from jax.experimental import pallas as pl
from jax.experimental.pallas import tpu as pltpu
from jax.sharding import PartitionSpec as P

MESH = pl.DeviceIdType.MESH
ORDER = (
    ("X", 1, 0), ("I", 1, 0, 0), ("X", 0, 1), ("I", 0, -1, 0), ("I", 0, 1, 0), ("X", 0, -1),
    ("I", 0, 0, 1), ("I", 0, 0, -1), ("X", 1, 1), ("X", 1, -1), ("I", 1, 0, -1), ("I", 1, 1, 0),
    ("I", 1, -1, 0), ("X", 0, -2), ("I", 1, 0, 1), ("I", 0, 2, 0), ("X", 0, 2), ("I", 0, -1, 1),
    ("I", 0, -1, -1), ("I", 0, 1, -1), ("I", 0, 1, 1), ("I", 0, 0, 2), ("X", 1, 2), ("X", 1, -2),
    ("I", 1, 1, 1), ("I", 1, -1, 1), ("X", 0, -3), ("X", 0, 3), ("I", 1, 1, -1), ("I", 1, 0, 2),
    ("I", 1, 2, 0), ("I", 1, -1, -1), ("I", 1, 1, 2), ("X", 1, 3), ("I", 0, 2, 1), ("X", 1, -3),
    ("I", 1, -1, 2), ("I", 0, 2, -1), ("X", 0, 4), ("I", 1, 2, -1), ("I", 1, 2, 1), ("I", 0, -1, 2),
    ("own",), ("X", 1, 4), ("I", 0, 1, 2), ("I", 1, 2, 2), ("I", 0, 2, 2), ("comp", 1),
    ("A", 0, -1, 0), ("A", 0, 1, 0), ("A", 0, 0, 1), ("A", 0, 0, -1), ("A", 1, 0, 0), ("comp", 0),
    ("T", 1, 1), ("T", 1, -1), ("A", 1, 0, 1), ("A", 1, 1, 0), ("A", 1, -1, 0), ("A", 1, 0, -1),
    ("A", 0, 2, 0), ("T", 0, -1), ("T", 0, 1), ("A", 0, -1, 1), ("A", 0, -1, -1), ("A", 0, 1, -1),
    ("A", 0, 1, 1), ("A", 1, 0, 2), ("T", 1, -2), ("T", 1, 2), ("A", 0, 0, 2), ("A", 1, 1, -1),
    ("T", 0, -2), ("T", 0, 2), ("A", 1, 1, 1), ("A", 1, 2, 0), ("A", 1, -1, 1), ("A", 1, -1, -1),
    ("T", 1, 3), ("T", 1, -3), ("A", 0, 2, 1), ("A", 0, 2, -1), ("A", 1, 1, 2), ("A", 0, -1, 2),
    ("A", 1, 2, 1), ("T", 0, -3), ("T", 0, 3), ("A", 1, 2, -1), ("A", 1, -1, 2), ("A", 0, 1, 2),
    ("A", 1, 2, 2), ("T", 1, 4), ("A", 0, 2, 2), ("R", 1), ("R", -3), ("R", 2), ("R", -2), ("R", 0),
    ("R", -1), ("R", 3), ("T", 0, 4), ("R", 4),
)


def split(v):
    high = v.astype(jnp.bfloat16)
    return high, (v - high.astype(jnp.float32)).astype(jnp.bfloat16)


def product(a, b):
    dot = functools.partial(jnp.dot, preferred_element_type=jnp.float32)
    return dot(a[0], b[0]) + (dot(a[0], b[1]) + dot(a[1], b[0]))


def kernel(
    nx, ny, nz, a_ref, i_ref, o_ref,
    x_rows, i_cols, a_cols, t_rows, total, theirs,
    x_high, x_low, i_high, i_low, a_high, a_low, t_high, t_low,
    send_sem, x_sem, i_sem, a_sem, t_sem, r_sem,
):
    rows = a_ref.shape[1]
    width = a_ref.shape[2]
    pair, z = lax.axis_index("pair"), lax.axis_index("int")
    c = lax.rem(pair, 2)
    chip = pair // 2
    y, x = lax.rem(chip, ny), chip // ny
    here = chip
    s = 1 - 2 * c
    parts = (c, 1 - c)

    def device(dx, dy, dz, core):
        xx, yy = lax.rem(x + dx + nx, nx), lax.rem(y + dy + ny, ny)
        zz = lax.rem(z + dz + nz, nz)
        return {"pair": (xx * ny + yy) * 2 + core, "int": zz}

    sibling = device(0, 0, 0, 1 - c)
    peers = [sibling]
    for core in (0, 1):
        for d in (1, -1):
            peers += [device(d, 0, 0, core), device(0, d, 0, core), device(0, 0, d, core)]
    barrier = pltpu.get_barrier_semaphore()
    for peer in peers:
        pl.semaphore_signal(barrier, inc=1, device_id=peer, device_id_type=MESH)
    pl.semaphore_wait(barrier, len(peers))

    started = []

    def send(src, dst, sem, to):
        copy = pltpu.make_async_remote_copy(
            src_ref=src, dst_ref=dst, send_sem=send_sem.at[len(started)], recv_sem=sem,
            device_id=to, device_id_type=MESH,
        )
        copy.start()
        started.append(copy)

    def arrived(ref, sem):
        pltpu.make_async_remote_copy(
            src_ref=ref, dst_ref=ref, send_sem=send_sem.at[0], recv_sem=sem,
            device_id=sibling, device_id_type=MESH,
        ).wait_recv()

    def keep(v, high, low, at, part):
        high[at, part], low[at, part] = split(v)

    def zs(d):
        return lax.rem(z + d + nz, nz)

    far = nz // 2

    def z_first():
        slot, sem = x_rows.at[z, c], x_sem.at[c, z]
        for d in (s, -s):
            for h in (c, 1 - c):
                send(a_ref.at[h], slot, sem, device(0, 0, d, h))
        send(a_ref.at[1 - c], slot, sem, sibling)
        keep(a_ref[c], x_high, x_low, z, c)

    def z_event(buf, sems, high, low, own, k):
        at, part = zs(-s * k), parts[own]
        slot, sem = buf.at[at, part], sems.at[part, at]
        arrived(slot, sem)
        if 0 < k < far:
            send(slot, slot, sem, device(0, 0, s, c))
        elif 1 - far < k < 0:
            send(slot, slot, sem, device(0, 0, -s, c))
        keep(buf[at, part], high, low, at, part)

    def turn(part, first, second):
        return first * (1 - part) + second * part, first * part + second * (1 - part)

    def xy_own(ref, buf, sems, high, low):
        slot, sem = buf.at[here, c], sems.at[c, here]

        def out(first, second):
            dx, dy = turn(c, first, second)
            for h in (c, 1 - c):
                send(ref.at[h], slot, sem, device(dx, dy, 0, h))

        out(s, 0)
        out(-s, 0)
        send(ref.at[1 - c], slot, sem, sibling)
        out(0, s)
        out(0, -s)
        keep(ref[c], high, low, here, c)

    def xy_event(buf, sems, high, low, own, first, second):
        part = parts[own]
        dx, dy = turn(part, s * first, s * second)
        at = lax.rem(x - dx + nx, nx) * ny + lax.rem(y - dy + ny, ny)
        slot, sem = buf.at[at, part], sems.at[part, at]
        arrived(slot, sem)
        along = []
        if second == 0 and first != 0:
            along = [(s, 0)] if first == 1 else []
            along += [(0, s), (0, -s)]
        elif second == 1:
            along = [(0, s)]
        for f, g in along:
            dx, dy = turn(part, f, g)
            send(slot, slot, sem, device(dx, dy, 0, c))
        keep(buf[at, part], high, low, at, part)

    def block(buf, k):
        return buf[pl.ds(2 * k, 2)].reshape(width, width)

    def t_event(own):
        part = parts[own]
        at = pl.ds(pl.multiple_of(part * rows, rows), rows)
        value = i_ref[c] if own == 0 else i_cols[here, part]
        for k in range(nz):
            value += product(
                (x_high[k, part], x_low[k, part]), (block(i_high, k), block(i_low, k))
            )
        total[at, :] = value
        t_rows[z, part] = value
        slot, sem = t_rows.at[z, part], t_sem.at[part, z]
        send(slot, slot, sem, device(0, 0, s, c))
        send(slot, slot, sem, device(0, 0, -s, c))
        keep(value, t_high, t_low, z, part)

    def r_event(k):
        at = zs(-s * k)
        t = [v[at].reshape(2 * rows, width) for v in (t_high, t_low)]
        total[...] += product(t, (block(a_high, at), block(a_low, at)))

    z_first()
    xy_own(i_ref, i_cols, i_sem, i_high, i_low)
    for name, *what in ORDER:
        if name == "X":
            z_event(x_rows, x_sem, x_high, x_low, *what)
        elif name == "T":
            z_event(t_rows, t_sem, t_high, t_low, *what)
        elif name == "I":
            xy_event(i_cols, i_sem, i_high, i_low, *what)
        elif name == "A":
            xy_event(a_cols, a_sem, a_high, a_low, *what)
        elif name == "own":
            xy_own(a_ref, a_cols, a_sem, a_high, a_low)
        elif name == "comp":
            t_event(*what)
        else:
            r_event(*what)
    part = pl.ds(pl.multiple_of((1 - c) * rows, rows), rows)
    send(total.at[part], theirs, r_sem, sibling)
    o_ref[c] = total[pl.ds(pl.multiple_of(c * rows, rows), rows), :]
    arrived(theirs, r_sem)
    o_ref[1 - c] = theirs[...]
    for copy in started:
        copy.wait_send()


def shards(amplitudes, integrals, nx, ny, nz):
    classes, rows, width = amplitudes.shape
    f32, b16 = jnp.float32, jnp.bfloat16
    dma = pltpu.SemaphoreType.DMA
    return pl.pallas_call(
        functools.partial(kernel, nx, ny, nz),
        out_shape=jax.ShapeDtypeStruct(amplitudes.shape, f32),
        in_specs=[pl.BlockSpec(memory_space=pltpu.VMEM)] * 2,
        out_specs=pl.BlockSpec(memory_space=pltpu.VMEM),
        scratch_shapes=[
            pltpu.VMEM((nz, 2, rows, width), f32),
            pltpu.VMEM((nx * ny, 2, rows, width), f32),
            pltpu.VMEM((nx * ny, 2, rows, width), f32),
            pltpu.VMEM((nz, 2, rows, width), f32),
            pltpu.VMEM((2 * rows, width), f32),
            pltpu.VMEM((rows, width), f32),
            pltpu.VMEM((nz, 2, rows, width), b16),
            pltpu.VMEM((nz, 2, rows, width), b16),
            pltpu.VMEM((nx * ny, 2, rows, width), b16),
            pltpu.VMEM((nx * ny, 2, rows, width), b16),
            pltpu.VMEM((nx * ny, 2, rows, width), b16),
            pltpu.VMEM((nx * ny, 2, rows, width), b16),
            pltpu.VMEM((nz, 2, rows, width), b16),
            pltpu.VMEM((nz, 2, rows, width), b16),
            dma((128,)),
            dma((2, nz)),
            dma((2, nx * ny)),
            dma((2, nx * ny)),
            dma((2, nz)),
            dma,
        ],
        compiler_params=pltpu.CompilerParams(
            collective_id=0, has_side_effects=True, vmem_limit_bytes=48 * 1024 * 1024
        ),
    )(amplitudes, integrals)


def solution(mesh):
    nz = mesh.shape["int"]
    nx = ny = 4
    placed = P(None, "pair", "int")
    return jax.shard_map(
        functools.partial(shards, nx=nx, ny=ny, nz=nz),
        mesh=mesh, in_specs=(placed, placed), out_specs=placed, check_vma=False,
    )
```

```python
import functools

import jax
import jax.numpy as jnp
from jax import lax
from jax.experimental import pallas as pl
from jax.experimental.pallas import tpu as pltpu
from jax.sharding import PartitionSpec as P

MESH = pl.DeviceIdType.MESH
ORDER = (
    ("own", "I", 1), ("own", "X"), ("own", "I", 2), ("I", 0, 1, 0), ("I", 1, 1, 0), ("I", 0, -1, 0),
    ("X", 1, -1), ("X", 1, 1), ("X", 0, -1), ("X", 0, 1), ("I", 1, -1, 0), ("I", 0, 0, -1),
    ("I", 0, 2, 0), ("I", 1, 0, -1), ("X", 1, -2), ("I", 0, 1, -1), ("I", 0, 1, 1), ("I", 1, 2, 0),
    ("X", 1, 2), ("I", 1, 1, 1), ("I", 0, -1, 1), ("X", 0, 2), ("I", 1, -1, 1), ("X", 0, -2),
    ("I", 0, -1, -1), ("I", 0, 0, 1), ("I", 1, 0, 1), ("I", 0, 2, 1), ("X", 1, -3), ("X", 1, 3),
    ("I", 1, 2, 1), ("X", 1, 0), ("X", 0, 3), ("I", 1, 1, -1), ("own", "A", 1), ("I", 0, 1, 2),
    ("I", 1, 0, 0), ("I", 0, 2, -1), ("I", 1, 2, -1), ("I", 1, 1, 2), ("own", "A", 2),
    ("I", 1, -1, 2), ("X", 0, -3), ("I", 0, -1, 2), ("X", 1, 4), ("I", 1, -1, -1), ("I", 1, 0, 2),
    ("I", 0, 0, 2), ("X", 0, 4), ("I", 1, 2, 2), ("I", 0, 2, 2), ("comp", 1), ("A", 0, 1, 0),
    ("comp", 0), ("A", 1, 1, 0), ("A", 0, -1, 0), ("T", 1, 1), ("T", 0, 1), ("A", 0, 2, 0),
    ("T", 0, -1), ("A", 1, -1, 0), ("A", 1, 2, 0), ("A", 1, 1, 1), ("A", 0, 0, -1), ("T", 1, -1),
    ("A", 1, 0, 1), ("A", 0, -1, 1), ("A", 0, 1, -1), ("T", 1, 2), ("T", 0, 2), ("A", 0, 1, 1),
    ("A", 0, -1, -1), ("T", 0, -2), ("A", 1, -1, 1), ("A", 1, 2, 1), ("T", 1, -2), ("A", 0, 0, 1),
    ("A", 1, 0, -1), ("A", 1, -1, -1), ("A", 0, 2, -1), ("A", 1, 1, -1), ("A", 0, 2, 1),
    ("A", 0, -1, 2), ("A", 1, 2, -1), ("A", 1, 0, 0), ("T", 1, 3), ("A", 1, 0, 2), ("T", 0, 3),
    ("T", 0, -3), ("A", 1, 1, 2), ("A", 0, 1, 2), ("A", 1, -1, 2), ("A", 0, 0, 2), ("T", 1, -3),
    ("A", 1, 2, 2), ("A", 0, 2, 2), ("R", -1), ("R", 3), ("R", 2), ("R", 0), ("R", -3), ("R", 1),
    ("T", 1, 4), ("R", -2), ("T", 0, 4), ("R", 4),
)


def split(v):
    high = v.astype(jnp.bfloat16)
    return high, (v - high.astype(jnp.float32)).astype(jnp.bfloat16)


def product(a, b):
    dot = functools.partial(jnp.dot, preferred_element_type=jnp.float32)
    return dot(a[0], b[0]) + (dot(a[0], b[1]) + dot(a[1], b[0]))


def kernel(
    nx, ny, nz, a_ref, i_ref, o_ref,
    x_rows, i_cols, a_cols, t_rows, total, theirs,
    x_high, x_low, i_high, i_low, a_high, a_low, t_high, t_low,
    send_sem, x_sem, i_sem, a_sem, t_sem, r_sem,
):
    rows = a_ref.shape[1]
    width = a_ref.shape[2]
    pair, z = lax.axis_index("pair"), lax.axis_index("int")
    c = lax.rem(pair, 2)
    chip = pair // 2
    y, x = lax.rem(chip, ny), chip // ny
    here = chip
    s = 1 - 2 * c
    parts = (c, 1 - c)

    def device(dx, dy, dz, core):
        xx, yy = lax.rem(x + dx + nx, nx), lax.rem(y + dy + ny, ny)
        zz = lax.rem(z + dz + nz, nz)
        return {"pair": (xx * ny + yy) * 2 + core, "int": zz}

    sibling = device(0, 0, 0, 1 - c)
    peers = [sibling]
    for core in (0, 1):
        for d in (1, -1):
            peers += [device(d, 0, 0, core), device(0, d, 0, core), device(0, 0, d, core)]
    barrier = pltpu.get_barrier_semaphore()
    for peer in peers:
        pl.semaphore_signal(barrier, inc=1, device_id=peer, device_id_type=MESH)
    pl.semaphore_wait(barrier, len(peers))

    started = []

    def send(src, dst, sem, to):
        copy = pltpu.make_async_remote_copy(
            src_ref=src, dst_ref=dst, send_sem=send_sem.at[len(started)], recv_sem=sem,
            device_id=to, device_id_type=MESH,
        )
        copy.start()
        started.append(copy)

    def arrived(ref, sem):
        pltpu.make_async_remote_copy(
            src_ref=ref, dst_ref=ref, send_sem=send_sem.at[0], recv_sem=sem,
            device_id=sibling, device_id_type=MESH,
        ).wait_recv()

    def keep(v, high, low, at, part):
        high[at, part], low[at, part] = split(v)

    def zs(d):
        return lax.rem(z + d + nz, nz)

    far = nz // 2

    def z_first():
        slot, sem = x_rows.at[z, c], x_sem.at[c, z]
        for d in (s, -s):
            for h in (c, 1 - c):
                send(a_ref.at[h], slot, sem, device(0, 0, d, h))
        send(a_ref.at[1 - c], slot, sem, sibling)
        keep(a_ref[c], x_high, x_low, z, c)

    def z_event(buf, sems, high, low, own, k):
        at, part = zs(-s * k), parts[own]
        slot, sem = buf.at[at, part], sems.at[part, at]
        arrived(slot, sem)
        if 0 < k < far:
            send(slot, slot, sem, device(0, 0, s, c))
        elif 1 - far < k < 0:
            send(slot, slot, sem, device(0, 0, -s, c))
        keep(buf[at, part], high, low, at, part)

    def turn(part, first, second):
        return first * (1 - part) + second * part, first * part + second * (1 - part)

    def xy_own(ref, buf, sems, high, low, leg):
        slot, sem = buf.at[here, c], sems.at[c, here]
        for d in (s, -s):
            dx, dy = turn(c, d, 0) if leg == 1 else turn(c, 0, d)
            for h in (c, 1 - c):
                send(ref.at[h], slot, sem, device(dx, dy, 0, h))
        if leg == 1:
            send(ref.at[1 - c], slot, sem, sibling)
            keep(ref[c], high, low, here, c)

    def xy_event(buf, sems, high, low, own, first, second):
        part = parts[own]
        dx, dy = turn(part, s * first, s * second)
        at = lax.rem(x - dx + nx, nx) * ny + lax.rem(y - dy + ny, ny)
        slot, sem = buf.at[at, part], sems.at[part, at]
        arrived(slot, sem)
        along = []
        if second == 0 and first != 0:
            along = [(s, 0)] if first == 1 else []
            along += [(0, s), (0, -s)]
        elif second == 1:
            along = [(0, s)]
        for f, g in along:
            dx, dy = turn(part, f, g)
            send(slot, slot, sem, device(dx, dy, 0, c))
        keep(buf[at, part], high, low, at, part)

    def block(buf, k):
        return buf[pl.ds(2 * k, 2)].reshape(width, width)

    def t_event(own):
        part = parts[own]
        at = pl.ds(pl.multiple_of(part * rows, rows), rows)
        value = i_ref[c] if own == 0 else i_cols[here, part]
        for k in range(nz):
            value += product(
                (x_high[k, part], x_low[k, part]), (block(i_high, k), block(i_low, k))
            )
        total[at, :] = value
        t_rows[z, part] = value
        slot, sem = t_rows.at[z, part], t_sem.at[part, z]
        send(slot, slot, sem, device(0, 0, s, c))
        send(slot, slot, sem, device(0, 0, -s, c))
        keep(value, t_high, t_low, z, part)

    def r_event(k):
        at = zs(-s * k)
        t = [v[at].reshape(2 * rows, width) for v in (t_high, t_low)]
        total[...] += product(t, (block(a_high, at), block(a_low, at)))

    i_all = (i_cols, i_sem, i_high, i_low)
    a_all = (a_cols, a_sem, a_high, a_low)
    for name, *what in ORDER:
        if name == "X":
            z_event(x_rows, x_sem, x_high, x_low, *what)
        elif name == "T":
            z_event(t_rows, t_sem, t_high, t_low, *what)
        elif name == "I":
            xy_event(*i_all, *what)
        elif name == "A":
            xy_event(*a_all, *what)
        elif name == "own" and what[0] == "X":
            z_first()
        elif name == "own" and what[0] == "I":
            xy_own(i_ref, *i_all, what[1])
        elif name == "own":
            xy_own(a_ref, *a_all, what[1])
        elif name == "comp":
            t_event(*what)
        else:
            r_event(*what)
    part = pl.ds(pl.multiple_of((1 - c) * rows, rows), rows)
    send(total.at[part], theirs, r_sem, sibling)
    o_ref[c] = total[pl.ds(pl.multiple_of(c * rows, rows), rows), :]
    arrived(theirs, r_sem)
    o_ref[1 - c] = theirs[...]
    for copy in started:
        copy.wait_send()


def shards(amplitudes, integrals, nx, ny, nz):
    classes, rows, width = amplitudes.shape
    f32, b16 = jnp.float32, jnp.bfloat16
    dma = pltpu.SemaphoreType.DMA
    return pl.pallas_call(
        functools.partial(kernel, nx, ny, nz),
        out_shape=jax.ShapeDtypeStruct(amplitudes.shape, f32),
        in_specs=[pl.BlockSpec(memory_space=pltpu.VMEM)] * 2,
        out_specs=pl.BlockSpec(memory_space=pltpu.VMEM),
        scratch_shapes=[
            pltpu.VMEM((nz, 2, rows, width), f32),
            pltpu.VMEM((nx * ny, 2, rows, width), f32),
            pltpu.VMEM((nx * ny, 2, rows, width), f32),
            pltpu.VMEM((nz, 2, rows, width), f32),
            pltpu.VMEM((2 * rows, width), f32),
            pltpu.VMEM((rows, width), f32),
            pltpu.VMEM((nz, 2, rows, width), b16),
            pltpu.VMEM((nz, 2, rows, width), b16),
            pltpu.VMEM((nx * ny, 2, rows, width), b16),
            pltpu.VMEM((nx * ny, 2, rows, width), b16),
            pltpu.VMEM((nx * ny, 2, rows, width), b16),
            pltpu.VMEM((nx * ny, 2, rows, width), b16),
            pltpu.VMEM((nz, 2, rows, width), b16),
            pltpu.VMEM((nz, 2, rows, width), b16),
            dma((128,)),
            dma((2, nz)),
            dma((2, nx * ny)),
            dma((2, nx * ny)),
            dma((2, nz)),
            dma,
        ],
        compiler_params=pltpu.CompilerParams(
            collective_id=0, has_side_effects=True, vmem_limit_bytes=48 * 1024 * 1024
        ),
    )(amplitudes, integrals)


def solution(mesh):
    nz = mesh.shape["int"]
    nx = ny = 4
    placed = P(None, "pair", "int")
    return jax.shard_map(
        functools.partial(shards, nx=nx, ny=ny, nz=nz),
        mesh=mesh, in_specs=(placed, placed), out_specs=placed, check_vma=False,
    )
```

```python
import functools

import jax
import jax.numpy as jnp
from jax import lax
from jax.experimental import pallas as pl
from jax.experimental.pallas import tpu as pltpu
from jax.sharding import PartitionSpec as P

MESH = pl.DeviceIdType.MESH
ORDER = (
    ("own", "I", 2), ("own", "I", 1), ("own", "X"), ("I", 0, 1, 0), ("X", 0, -1), ("X", 0, 1),
    ("I", 1, 1, 0), ("I", 1, -1, 0), ("X", 1, -1), ("I", 0, -1, 0), ("X", 1, 1), ("X", 0, -2),
    ("I", 0, 2, 0), ("X", 0, 2), ("I", 1, 2, 0), ("X", 1, 2), ("I", 1, 0, 0), ("X", 1, 0),
    ("I", 0, -1, -1), ("X", 1, -2), ("I", 0, 0, 1), ("I", 1, 1, 1), ("I", 0, 0, -1),
    ("I", 1, -1, -1), ("I", 1, 0, 1), ("I", 0, 1, 1), ("I", 1, 1, -1), ("X", 0, 3), ("I", 0, 2, 1),
    ("I", 0, 1, -1), ("I", 1, 2, 1), ("I", 0, 2, -1), ("X", 1, 3), ("I", 0, -1, 1), ("I", 1, 0, -1),
    ("own", "A", 2), ("I", 1, -1, 1), ("own", "A", 1), ("X", 0, -3), ("I", 1, -1, 2),
    ("I", 0, -1, 2), ("I", 1, 2, -1), ("I", 0, 0, 2), ("A", 1, 0, 0), ("I", 1, 0, 2), ("X", 1, -3),
    ("X", 0, 4), ("I", 0, 1, 2), ("X", 1, 4), ("I", 1, 1, 2), ("I", 0, 2, 2), ("I", 1, 2, 2),
    ("comp", 1), ("A", 0, 1, 0), ("comp", 0), ("A", 1, 1, 0), ("A", 0, -1, 0), ("A", 1, -1, 0),
    ("T", 1, 1), ("T", 1, -1), ("T", 0, 1), ("A", 0, 1, 1), ("A", 0, 0, -1), ("A", 0, 2, 0),
    ("A", 1, 1, 1), ("A", 1, 2, 0), ("T", 0, -1), ("A", 1, 1, -1), ("A", 1, 0, 1), ("T", 1, 2),
    ("A", 0, 0, 1), ("A", 0, 1, -1), ("A", 0, -1, -1), ("T", 0, 2), ("A", 1, -1, -1), ("T", 1, -2),
    ("A", 0, 2, 1), ("A", 1, 2, 1), ("A", 0, -1, 1), ("T", 0, -2), ("T", 1, 3), ("A", 1, 0, -1),
    ("A", 1, 1, 2), ("A", 0, 2, -1), ("T", 0, 3), ("A", 0, 1, 2), ("A", 0, -1, 2), ("A", 1, 2, -1),
    ("A", 1, -1, 1), ("A", 0, 0, 2), ("A", 1, 2, 2), ("A", 0, 2, 2), ("A", 1, -1, 2), ("T", 1, -3),
    ("A", 1, 0, 2), ("T", 0, -3), ("R", 2), ("R", -2), ("R", 0), ("R", -1), ("R", 1), ("R", 3),
    ("R", -3), ("T", 1, 4), ("T", 0, 4), ("R", 4),
)


def split(v):
    high = v.astype(jnp.bfloat16)
    return high, (v - high.astype(jnp.float32)).astype(jnp.bfloat16)


def product(a, b):
    dot = functools.partial(jnp.dot, preferred_element_type=jnp.float32)
    return dot(a[0], b[0]) + (dot(a[0], b[1]) + dot(a[1], b[0]))


def kernel(
    nx, ny, nz, a_ref, i_ref, o_ref,
    x_rows, i_cols, a_cols, t_rows, total, theirs,
    x_high, x_low, i_high, i_low, a_high, a_low, t_high, t_low,
    send_sem, x_sem, i_sem, a_sem, t_sem, r_sem,
):
    rows = a_ref.shape[1]
    width = a_ref.shape[2]
    pair, z = lax.axis_index("pair"), lax.axis_index("int")
    c = lax.rem(pair, 2)
    chip = pair // 2
    y, x = lax.rem(chip, ny), chip // ny
    here = chip
    s = 1 - 2 * c
    parts = (c, 1 - c)

    def device(dx, dy, dz, core):
        xx, yy = lax.rem(x + dx + nx, nx), lax.rem(y + dy + ny, ny)
        zz = lax.rem(z + dz + nz, nz)
        return {"pair": (xx * ny + yy) * 2 + core, "int": zz}

    sibling = device(0, 0, 0, 1 - c)
    peers = [sibling]
    for core in (0, 1):
        for d in (1, -1):
            peers += [device(d, 0, 0, core), device(0, d, 0, core), device(0, 0, d, core)]
    barrier = pltpu.get_barrier_semaphore()
    for peer in peers:
        pl.semaphore_signal(barrier, inc=1, device_id=peer, device_id_type=MESH)
    pl.semaphore_wait(barrier, len(peers))

    started = []

    def send(src, dst, sem, to):
        copy = pltpu.make_async_remote_copy(
            src_ref=src, dst_ref=dst, send_sem=send_sem.at[len(started)], recv_sem=sem,
            device_id=to, device_id_type=MESH,
        )
        copy.start()
        started.append(copy)

    def arrived(ref, sem):
        pltpu.make_async_remote_copy(
            src_ref=ref, dst_ref=ref, send_sem=send_sem.at[0], recv_sem=sem,
            device_id=sibling, device_id_type=MESH,
        ).wait_recv()

    def keep(v, high, low, at, part):
        high[at, part], low[at, part] = split(v)

    def zs(d):
        return lax.rem(z + d + nz, nz)

    far = nz // 2

    def z_first():
        slot, sem = x_rows.at[z, c], x_sem.at[c, z]
        for d in (s, -s):
            for h in (c, 1 - c):
                send(a_ref.at[h], slot, sem, device(0, 0, d, h))
        send(a_ref.at[1 - c], slot, sem, sibling)
        keep(a_ref[c], x_high, x_low, z, c)

    def z_event(buf, sems, high, low, own, k):
        part = parts[own]
        way = 1 - 2 * part
        at = zs(-way * k)
        slot, sem = buf.at[at, part], sems.at[part, at]
        arrived(slot, sem)
        if 0 < k < far:
            send(slot, slot, sem, device(0, 0, way, c))
        elif 1 - far < k < 0:
            send(slot, slot, sem, device(0, 0, -way, c))
        keep(buf[at, part], high, low, at, part)

    def turn(part, first, second):
        return first * (1 - part) + second * part, first * part + second * (1 - part)

    def xy_own(ref, buf, sems, high, low, leg):
        slot, sem = buf.at[here, c], sems.at[c, here]
        for d in (s, -s):
            dx, dy = turn(c, d, 0) if leg == 1 else turn(c, 0, d)
            for h in (c, 1 - c):
                send(ref.at[h], slot, sem, device(dx, dy, 0, h))
        if leg == 1:
            send(ref.at[1 - c], slot, sem, sibling)
            keep(ref[c], high, low, here, c)

    def xy_event(buf, sems, high, low, own, first, second):
        part = parts[own]
        dx, dy = turn(part, s * first, s * second)
        at = lax.rem(x - dx + nx, nx) * ny + lax.rem(y - dy + ny, ny)
        slot, sem = buf.at[at, part], sems.at[part, at]
        arrived(slot, sem)
        along = []
        if second == 0 and first != 0:
            along = [(s, 0)] if first == 1 else []
            along += [(0, s), (0, -s)]
        elif second == (1 if first in (0, 2) else -1):
            along = [(0, second * s)]
        for f, g in along:
            dx, dy = turn(part, f, g)
            send(slot, slot, sem, device(dx, dy, 0, c))
        keep(buf[at, part], high, low, at, part)

    def block(buf, k):
        return buf[pl.ds(2 * k, 2)].reshape(width, width)

    def t_event(own):
        part = parts[own]
        at = pl.ds(pl.multiple_of(part * rows, rows), rows)
        value = i_ref[c] if own == 0 else i_cols[here, part]
        for k in range(nz):
            value += product(
                (x_high[k, part], x_low[k, part]), (block(i_high, k), block(i_low, k))
            )
        total[at, :] = value
        t_rows[z, part] = value
        slot, sem = t_rows.at[z, part], t_sem.at[part, z]
        way = 1 - 2 * part
        send(slot, slot, sem, device(0, 0, way, c))
        send(slot, slot, sem, device(0, 0, -way, c))
        keep(value, t_high, t_low, z, part)

    def r_event(k, own=1):
        at, part = zs(-s * k), parts[own]
        here_rows = pl.ds(pl.multiple_of(part * rows, rows), rows)
        total[here_rows, :] += product(
            (t_high[at, part], t_low[at, part]), (block(a_high, at), block(a_low, at))
        )

    i_all = (i_cols, i_sem, i_high, i_low)
    a_all = (a_cols, a_sem, a_high, a_low)
    for name, *what in ORDER:
        if name == "X":
            z_event(x_rows, x_sem, x_high, x_low, *what)
        elif name == "T":
            z_event(t_rows, t_sem, t_high, t_low, *what)
        elif name == "I":
            xy_event(*i_all, *what)
        elif name == "A":
            xy_event(*a_all, *what)
        elif name == "own" and what[0] == "X":
            z_first()
        elif name == "own" and what[0] == "I":
            xy_own(i_ref, *i_all, what[1])
        elif name == "own":
            xy_own(a_ref, *a_all, what[1])
        elif name == "comp":
            t_event(*what)
        else:
            r_event(*what)
    part = pl.ds(pl.multiple_of((1 - c) * rows, rows), rows)
    send(total.at[part], theirs, r_sem, sibling)
    for name, *what in ORDER:
        if name == "R":
            r_event(*what, own=0)
    o_ref[c] = total[pl.ds(pl.multiple_of(c * rows, rows), rows), :]
    arrived(theirs, r_sem)
    o_ref[1 - c] = theirs[...]
    for copy in started:
        copy.wait_send()


def shards(amplitudes, integrals, nx, ny, nz):
    classes, rows, width = amplitudes.shape
    f32, b16 = jnp.float32, jnp.bfloat16
    dma = pltpu.SemaphoreType.DMA
    return pl.pallas_call(
        functools.partial(kernel, nx, ny, nz),
        out_shape=jax.ShapeDtypeStruct(amplitudes.shape, f32),
        in_specs=[pl.BlockSpec(memory_space=pltpu.VMEM)] * 2,
        out_specs=pl.BlockSpec(memory_space=pltpu.VMEM),
        scratch_shapes=[
            pltpu.VMEM((nz, 2, rows, width), f32),
            pltpu.VMEM((nx * ny, 2, rows, width), f32),
            pltpu.VMEM((nx * ny, 2, rows, width), f32),
            pltpu.VMEM((nz, 2, rows, width), f32),
            pltpu.VMEM((2 * rows, width), f32),
            pltpu.VMEM((rows, width), f32),
            pltpu.VMEM((nz, 2, rows, width), b16),
            pltpu.VMEM((nz, 2, rows, width), b16),
            pltpu.VMEM((nx * ny, 2, rows, width), b16),
            pltpu.VMEM((nx * ny, 2, rows, width), b16),
            pltpu.VMEM((nx * ny, 2, rows, width), b16),
            pltpu.VMEM((nx * ny, 2, rows, width), b16),
            pltpu.VMEM((nz, 2, rows, width), b16),
            pltpu.VMEM((nz, 2, rows, width), b16),
            dma((128,)),
            dma((2, nz)),
            dma((2, nx * ny)),
            dma((2, nx * ny)),
            dma((2, nz)),
            dma,
        ],
        compiler_params=pltpu.CompilerParams(
            collective_id=0, has_side_effects=True, vmem_limit_bytes=48 * 1024 * 1024
        ),
    )(amplitudes, integrals)


def solution(mesh):
    nz = mesh.shape["int"]
    nx = ny = 4
    placed = P(None, "pair", "int")
    return jax.shard_map(
        functools.partial(shards, nx=nx, ny=ny, nz=nz),
        mesh=mesh, in_specs=(placed, placed), out_specs=placed, check_vma=False,
    )
```

```python
import functools

import jax
import jax.numpy as jnp
from jax import lax
from jax.experimental import pallas as pl
from jax.experimental.pallas import tpu as pltpu
from jax.sharding import PartitionSpec as P

MESH = pl.DeviceIdType.MESH
ORDER = (
    ("own", "I", 2), ("own", "I", 1), ("own", "X"), ("I", 0, 1, 0), ("X", 0, -1), ("X", 0, 1),
    ("I", 1, 1, 0), ("I", 1, -1, 0), ("X", 1, -1), ("I", 0, -1, 0), ("X", 1, 1), ("X", 0, -2),
    ("I", 0, 2, 0), ("X", 0, 2), ("I", 1, 2, 0), ("X", 1, 2), ("I", 1, 0, 0), ("X", 1, 0),
    ("I", 0, -1, -1), ("X", 1, -2), ("I", 0, 0, 1), ("I", 1, 1, 1), ("I", 0, 0, -1),
    ("I", 1, -1, -1), ("I", 1, 0, 1), ("I", 0, 1, 1), ("I", 1, 1, -1), ("X", 0, 3), ("I", 0, 2, 1),
    ("I", 0, 1, -1), ("I", 1, 2, 1), ("I", 0, 2, -1), ("X", 1, 3), ("I", 0, -1, 1), ("I", 1, 0, -1),
    ("own", "A", 2), ("I", 1, -1, 1), ("own", "A", 1), ("X", 0, -3), ("I", 1, -1, 2),
    ("I", 0, -1, 2), ("I", 1, 2, -1), ("I", 0, 0, 2), ("A", 1, 0, 0), ("I", 1, 0, 2), ("X", 1, -3),
    ("X", 0, 4), ("I", 0, 1, 2), ("X", 1, 4), ("I", 1, 1, 2), ("I", 0, 2, 2), ("I", 1, 2, 2),
    ("comp", 1), ("A", 0, 1, 0), ("comp", 0), ("A", 1, 1, 0), ("A", 0, -1, 0), ("A", 1, -1, 0),
    ("T", 1, 1), ("T", 1, -1), ("T", 0, 1), ("A", 0, 1, 1), ("A", 0, 0, -1), ("A", 0, 2, 0),
    ("A", 1, 1, 1), ("A", 1, 2, 0), ("T", 0, -1), ("A", 1, 1, -1), ("A", 1, 0, 1), ("T", 1, 2),
    ("A", 0, 0, 1), ("A", 0, 1, -1), ("A", 0, -1, -1), ("T", 0, 2), ("A", 1, -1, -1), ("T", 1, -2),
    ("A", 0, 2, 1), ("A", 1, 2, 1), ("A", 0, -1, 1), ("T", 0, -2), ("T", 1, 3), ("A", 1, 0, -1),
    ("A", 1, 1, 2), ("A", 0, 2, -1), ("T", 0, 3), ("A", 0, 1, 2), ("A", 0, -1, 2), ("A", 1, 2, -1),
    ("A", 1, -1, 1), ("A", 0, 0, 2), ("A", 1, 2, 2), ("A", 0, 2, 2), ("A", 1, -1, 2), ("T", 1, -3),
    ("A", 1, 0, 2), ("T", 0, -3), ("R", 2), ("R", -2), ("R", 0), ("R", -1), ("R", 1), ("R", 3),
    ("R", -3), ("T", 1, 4), ("T", 0, 4), ("R", 4),
)


def split(v):
    high = v.astype(jnp.bfloat16)
    return high, (v - high.astype(jnp.float32)).astype(jnp.bfloat16)


def product(a, b):
    dot = functools.partial(jnp.dot, preferred_element_type=jnp.float32)
    n = a[0].shape[0]
    both = dot(jnp.concatenate(a, axis=0), b[0])
    return both[:n] + (dot(a[0], b[1]) + both[n:])


def kernel(
    nx, ny, nz, a_ref, i_ref, o_ref,
    x_rows, i_cols, a_cols, t_rows, total, theirs,
    x_high, x_low, i_high, i_low, a_high, a_low, t_high, t_low,
    send_sem, x_sem, i_sem, a_sem, t_sem, r_sem,
):
    rows = a_ref.shape[1]
    width = a_ref.shape[2]
    pair, z = lax.axis_index("pair"), lax.axis_index("int")
    c = lax.rem(pair, 2)
    chip = pair // 2
    y, x = lax.rem(chip, ny), chip // ny
    here = chip
    s = 1 - 2 * c
    parts = (c, 1 - c)

    def device(dx, dy, dz, core):
        xx, yy = lax.rem(x + dx + nx, nx), lax.rem(y + dy + ny, ny)
        zz = lax.rem(z + dz + nz, nz)
        return {"pair": (xx * ny + yy) * 2 + core, "int": zz}

    sibling = device(0, 0, 0, 1 - c)
    peers = [sibling]
    for core in (0, 1):
        for d in (1, -1):
            peers += [device(d, 0, 0, core), device(0, d, 0, core), device(0, 0, d, core)]
    barrier = pltpu.get_barrier_semaphore()
    for peer in peers:
        pl.semaphore_signal(barrier, inc=1, device_id=peer, device_id_type=MESH)
    pl.semaphore_wait(barrier, len(peers))

    started = []

    def send(src, dst, sem, to):
        copy = pltpu.make_async_remote_copy(
            src_ref=src, dst_ref=dst, send_sem=send_sem.at[len(started)], recv_sem=sem,
            device_id=to, device_id_type=MESH,
        )
        copy.start()
        started.append(copy)

    def arrived(ref, sem):
        pltpu.make_async_remote_copy(
            src_ref=ref, dst_ref=ref, send_sem=send_sem.at[0], recv_sem=sem,
            device_id=sibling, device_id_type=MESH,
        ).wait_recv()

    def keep(v, high, low, at, part):
        high[at, part], low[at, part] = split(v)

    def zs(d):
        return lax.rem(z + d + nz, nz)

    far = nz // 2
    pieces = ((slice(0, rows // 2), 0), (slice(rows // 2, rows), 1))

    def z_first():
        slot, sem = x_rows.at[z, c], x_sem.at[c, z, 0]
        for d in (s, -s):
            for h in (c, 1 - c):
                send(a_ref.at[h], slot, sem, device(0, 0, d, h))
        send(a_ref.at[1 - c], slot, sem, sibling)
        keep(a_ref[c], x_high, x_low, z, c)

    def z_event(buf, sems, high, low, own, k):
        part = parts[own]
        way = 1 - 2 * part
        at = zs(-way * k)
        for rows_at, half in pieces if buf is t_rows else ((slice(None), 0),):
            slot, sem = buf.at[at, part, rows_at], sems.at[part, at, half]
            arrived(slot, sem)
            if 0 < k < far:
                send(slot, slot, sem, device(0, 0, way, c))
            elif 1 - far < k < 0:
                send(slot, slot, sem, device(0, 0, -way, c))
        keep(buf[at, part], high, low, at, part)

    def turn(part, first, second):
        return first * (1 - part) + second * part, first * part + second * (1 - part)

    def xy_own(ref, buf, sems, high, low, leg):
        slot, sem = buf.at[here, c], sems.at[c, here]
        for d in (s, -s):
            dx, dy = turn(c, d, 0) if leg == 1 else turn(c, 0, d)
            for h in (c, 1 - c):
                send(ref.at[h], slot, sem, device(dx, dy, 0, h))
        if leg == 1:
            send(ref.at[1 - c], slot, sem, sibling)
            keep(ref[c], high, low, here, c)

    def xy_event(buf, sems, high, low, own, first, second):
        part = parts[own]
        dx, dy = turn(part, s * first, s * second)
        at = lax.rem(x - dx + nx, nx) * ny + lax.rem(y - dy + ny, ny)
        slot, sem = buf.at[at, part], sems.at[part, at]
        arrived(slot, sem)
        along = []
        if second == 0 and first != 0:
            along = [(s, 0)] if first == 1 else []
            along += [(0, s), (0, -s)]
        elif second == (1 if first in (0, 2) else -1):
            along = [(0, second * s)]
        for f, g in along:
            dx, dy = turn(part, f, g)
            send(slot, slot, sem, device(dx, dy, 0, c))
        keep(buf[at, part], high, low, at, part)

    def block(buf, k):
        return buf[pl.ds(2 * k, 2)].reshape(width, width)

    def t_event(own):
        part = parts[own]
        at = pl.ds(pl.multiple_of(part * rows, rows), rows)
        value = i_ref[c] if own == 0 else i_cols[here, part]
        for k in range(nz):
            value += product(
                (x_high[k, part], x_low[k, part]), (block(i_high, k), block(i_low, k))
            )
        total[at, :] = value
        t_rows[z, part] = value
        way = 1 - 2 * part
        for rows_at, half in pieces:
            slot, sem = t_rows.at[z, part, rows_at], t_sem.at[part, z, half]
            send(slot, slot, sem, device(0, 0, way, c))
            send(slot, slot, sem, device(0, 0, -way, c))
        keep(value, t_high, t_low, z, part)

    def r_event(k, own=1):
        at, part = zs(-s * k), parts[own]
        here_rows = pl.ds(pl.multiple_of(part * rows, rows), rows)
        total[here_rows, :] += product(
            (t_high[at, part], t_low[at, part]), (block(a_high, at), block(a_low, at))
        )

    i_all = (i_cols, i_sem, i_high, i_low)
    a_all = (a_cols, a_sem, a_high, a_low)
    for name, *what in ORDER:
        if name == "X":
            z_event(x_rows, x_sem, x_high, x_low, *what)
        elif name == "T":
            z_event(t_rows, t_sem, t_high, t_low, *what)
        elif name == "I":
            xy_event(*i_all, *what)
        elif name == "A":
            xy_event(*a_all, *what)
        elif name == "own" and what[0] == "X":
            z_first()
        elif name == "own" and what[0] == "I":
            xy_own(i_ref, *i_all, what[1])
        elif name == "own":
            xy_own(a_ref, *a_all, what[1])
        elif name == "comp":
            t_event(*what)
        else:
            r_event(*what)
    part = pl.ds(pl.multiple_of((1 - c) * rows, rows), rows)
    send(total.at[part], theirs, r_sem, sibling)
    for name, *what in ORDER:
        if name == "R":
            r_event(*what, own=0)
    o_ref[c] = total[pl.ds(pl.multiple_of(c * rows, rows), rows), :]
    arrived(theirs, r_sem)
    o_ref[1 - c] = theirs[...]
    for copy in started:
        copy.wait_send()


def shards(amplitudes, integrals, nx, ny, nz):
    classes, rows, width = amplitudes.shape
    f32, b16 = jnp.float32, jnp.bfloat16
    dma = pltpu.SemaphoreType.DMA
    return pl.pallas_call(
        functools.partial(kernel, nx, ny, nz),
        out_shape=jax.ShapeDtypeStruct(amplitudes.shape, f32),
        in_specs=[pl.BlockSpec(memory_space=pltpu.VMEM)] * 2,
        out_specs=pl.BlockSpec(memory_space=pltpu.VMEM),
        scratch_shapes=[
            pltpu.VMEM((nz, 2, rows, width), f32),
            pltpu.VMEM((nx * ny, 2, rows, width), f32),
            pltpu.VMEM((nx * ny, 2, rows, width), f32),
            pltpu.VMEM((nz, 2, rows, width), f32),
            pltpu.VMEM((2 * rows, width), f32),
            pltpu.VMEM((rows, width), f32),
            pltpu.VMEM((nz, 2, rows, width), b16),
            pltpu.VMEM((nz, 2, rows, width), b16),
            pltpu.VMEM((nx * ny, 2, rows, width), b16),
            pltpu.VMEM((nx * ny, 2, rows, width), b16),
            pltpu.VMEM((nx * ny, 2, rows, width), b16),
            pltpu.VMEM((nx * ny, 2, rows, width), b16),
            pltpu.VMEM((nz, 2, rows, width), b16),
            pltpu.VMEM((nz, 2, rows, width), b16),
            dma((160,)),
            dma((2, nz, 2)),
            dma((2, nx * ny)),
            dma((2, nx * ny)),
            dma((2, nz, 2)),
            dma,
        ],
        compiler_params=pltpu.CompilerParams(
            collective_id=0, has_side_effects=True, vmem_limit_bytes=48 * 1024 * 1024
        ),
    )(amplitudes, integrals)


def solution(mesh):
    nz = mesh.shape["int"]
    nx = ny = 4
    placed = P(None, "pair", "int")
    return jax.shard_map(
        functools.partial(shards, nx=nx, ny=ny, nz=nz),
        mesh=mesh, in_specs=(placed, placed), out_specs=placed, check_vma=False,
    )
```

```python
import functools

import jax
import jax.numpy as jnp
from jax import lax
from jax.experimental import pallas as pl
from jax.experimental.pallas import tpu as pltpu
from jax.sharding import PartitionSpec as P

MESH = pl.DeviceIdType.MESH
ORDER = (
    ("own", "I", 2), ("own", "I", 1), ("own", "X"), ("I", 0, 1, 0), ("X", 0, -1), ("X", 0, 1),
    ("I", 1, 1, 0), ("I", 1, -1, 0), ("X", 1, -1), ("I", 0, -1, 0), ("X", 1, 1), ("X", 0, -2),
    ("I", 0, 2, 0), ("X", 0, 2), ("I", 1, 2, 0), ("X", 1, 2), ("I", 1, 0, 0), ("X", 1, 0),
    ("I", 0, -1, -1), ("X", 1, -2), ("I", 0, 0, 1), ("I", 1, 1, 1), ("I", 0, 0, -1),
    ("I", 1, -1, -1), ("I", 1, 0, 1), ("I", 0, 1, 1), ("I", 1, 1, -1), ("X", 0, 3), ("I", 0, 2, 1),
    ("I", 0, 1, -1), ("I", 1, 2, 1), ("I", 0, 2, -1), ("X", 1, 3), ("I", 0, -1, 1), ("I", 1, 0, -1),
    ("own", "A", 2), ("I", 1, -1, 1), ("own", "A", 1), ("X", 0, -3), ("I", 1, -1, 2),
    ("I", 0, -1, 2), ("I", 1, 2, -1), ("I", 0, 0, 2), ("A", 1, 0, 0), ("I", 1, 0, 2), ("X", 1, -3),
    ("X", 0, 4), ("I", 0, 1, 2), ("X", 1, 4), ("I", 1, 1, 2), ("I", 0, 2, 2), ("I", 1, 2, 2),
    ("comp", 1), ("A", 0, 1, 0), ("comp", 0), ("A", 1, 1, 0), ("A", 0, -1, 0), ("A", 1, -1, 0),
    ("T", 1, 1), ("T", 1, -1), ("T", 0, 1), ("A", 0, 1, 1), ("A", 0, 0, -1), ("A", 0, 2, 0),
    ("A", 1, 1, 1), ("A", 1, 2, 0), ("T", 0, -1), ("A", 1, 1, -1), ("A", 1, 0, 1), ("T", 1, 2),
    ("A", 0, 0, 1), ("A", 0, 1, -1), ("A", 0, -1, -1), ("T", 0, 2), ("A", 1, -1, -1), ("T", 1, -2),
    ("A", 0, 2, 1), ("A", 1, 2, 1), ("A", 0, -1, 1), ("T", 0, -2), ("T", 1, 3), ("A", 1, 0, -1),
    ("A", 1, 1, 2), ("A", 0, 2, -1), ("T", 0, 3), ("A", 0, 1, 2), ("A", 0, -1, 2), ("A", 1, 2, -1),
    ("A", 1, -1, 1), ("A", 0, 0, 2), ("A", 1, 2, 2), ("A", 0, 2, 2), ("A", 1, -1, 2), ("T", 1, -3),
    ("A", 1, 0, 2), ("T", 0, -3), ("R", 2), ("R", -2), ("R", 0), ("R", -1), ("R", 1), ("R", 3),
    ("R", -3), ("T", 1, 4), ("T", 0, 4), ("R", 4),
)


def split(v):
    high = v.astype(jnp.bfloat16)
    return high, (v - high.astype(jnp.float32)).astype(jnp.bfloat16)


def product(a, b):
    dot = functools.partial(jnp.dot, preferred_element_type=jnp.float32)
    n = a[0].shape[0]
    both = dot(jnp.concatenate(a, axis=0), b[0])
    return both[:n] + (dot(a[0], b[1]) + both[n:])


def kernel(
    nx, ny, nz, a_ref, i_ref, o_ref,
    x_rows, i_cols, a_cols, t_rows, total,
    x_high, x_low, i_high, i_low, a_high, a_low, t_high, t_low,
    send_sem, x_sem, i_sem, a_sem, t_sem, r_sem,
):
    rows = a_ref.shape[1]
    width = a_ref.shape[2]
    pair, z = lax.axis_index("pair"), lax.axis_index("int")
    c = lax.rem(pair, 2)
    chip = pair // 2
    y, x = lax.rem(chip, ny), chip // ny
    here = chip
    s = 1 - 2 * c
    parts = (c, 1 - c)

    def device(dx, dy, dz, core):
        xx, yy = lax.rem(x + dx + nx, nx), lax.rem(y + dy + ny, ny)
        zz = lax.rem(z + dz + nz, nz)
        return {"pair": (xx * ny + yy) * 2 + core, "int": zz}

    sibling = device(0, 0, 0, 1 - c)
    peers = [sibling]
    for core in (0, 1):
        for d in (1, -1):
            peers += [device(d, 0, 0, core), device(0, d, 0, core), device(0, 0, d, core)]
    barrier = pltpu.get_barrier_semaphore()
    for peer in peers:
        pl.semaphore_signal(barrier, inc=1, device_id=peer, device_id_type=MESH)
    pl.semaphore_wait(barrier, len(peers))

    started = []

    def send(src, dst, sem, to):
        copy = pltpu.make_async_remote_copy(
            src_ref=src, dst_ref=dst, send_sem=send_sem.at[len(started)], recv_sem=sem,
            device_id=to, device_id_type=MESH,
        )
        copy.start()
        started.append(copy)

    def arrived(ref, sem):
        pltpu.make_async_remote_copy(
            src_ref=ref, dst_ref=ref, send_sem=send_sem.at[0], recv_sem=sem,
            device_id=sibling, device_id_type=MESH,
        ).wait_recv()

    def keep(v, high, low, at, part):
        high[at, part], low[at, part] = split(v)

    def zs(d):
        return lax.rem(z + d + nz, nz)

    far = nz // 2
    pieces = ((slice(0, rows // 2), 0), (slice(rows // 2, rows), 1))

    def z_first():
        slot, sem = x_rows.at[z, c], x_sem.at[c, z, 0]
        for d in (s, -s):
            for h in (c, 1 - c):
                send(a_ref.at[h], slot, sem, device(0, 0, d, h))
        send(a_ref.at[1 - c], slot, sem, sibling)
        keep(a_ref[c], x_high, x_low, z, c)

    def z_event(buf, sems, high, low, own, k):
        part = parts[own]
        way = 1 - 2 * part
        at = zs(-way * k)
        for rows_at, half in pieces if buf is t_rows else ((slice(None), 0),):
            slot, sem = buf.at[at, part, rows_at], sems.at[part, at, half]
            arrived(slot, sem)
            if 0 < k < far:
                send(slot, slot, sem, device(0, 0, way, c))
            elif 1 - far < k < 0:
                send(slot, slot, sem, device(0, 0, -way, c))
        keep(buf[at, part], high, low, at, part)

    def turn(part, first, second):
        return first * (1 - part) + second * part, first * part + second * (1 - part)

    def xy_own(ref, buf, sems, high, low, leg):
        slot, sem = buf.at[here, c], sems.at[c, here]
        for d in (s, -s):
            dx, dy = turn(c, d, 0) if leg == 1 else turn(c, 0, d)
            for h in (c, 1 - c):
                send(ref.at[h], slot, sem, device(dx, dy, 0, h))
        if leg == 1:
            send(ref.at[1 - c], slot, sem, sibling)
            keep(ref[c], high, low, here, c)

    def xy_event(buf, sems, high, low, own, first, second):
        part = parts[own]
        dx, dy = turn(part, s * first, s * second)
        at = lax.rem(x - dx + nx, nx) * ny + lax.rem(y - dy + ny, ny)
        slot, sem = buf.at[at, part], sems.at[part, at]
        arrived(slot, sem)
        along = []
        if second == 0 and first != 0:
            along = [(s, 0)] if first == 1 else []
            along += [(0, s), (0, -s)]
        elif second == (1 if first in (0, 2) else -1):
            along = [(0, second * s)]
        for f, g in along:
            dx, dy = turn(part, f, g)
            send(slot, slot, sem, device(dx, dy, 0, c))
        keep(buf[at, part], high, low, at, part)

    def block(buf, k):
        return buf[pl.ds(2 * k, 2)].reshape(width, width)

    def t_event(own):
        part = parts[own]
        at = pl.ds(pl.multiple_of(part * rows, rows), rows)
        value = i_ref[c] if own == 0 else i_cols[here, part]
        for k in range(nz):
            value += product(
                (x_high[k, part], x_low[k, part]), (block(i_high, k), block(i_low, k))
            )
        total[at, :] = value
        t_rows[z, part] = value
        way = 1 - 2 * part
        for rows_at, half in pieces:
            slot, sem = t_rows.at[z, part, rows_at], t_sem.at[part, z, half]
            send(slot, slot, sem, device(0, 0, way, c))
            send(slot, slot, sem, device(0, 0, -way, c))
        keep(value, t_high, t_low, z, part)

    def r_event(k, own=1):
        at, part = zs(-s * k), parts[own]
        here_rows = pl.ds(pl.multiple_of(part * rows, rows), rows)
        total[here_rows, :] += product(
            (t_high[at, part], t_low[at, part]), (block(a_high, at), block(a_low, at))
        )

    i_all = (i_cols, i_sem, i_high, i_low)
    a_all = (a_cols, a_sem, a_high, a_low)
    for name, *what in ORDER:
        if name == "X":
            z_event(x_rows, x_sem, x_high, x_low, *what)
        elif name == "T":
            z_event(t_rows, t_sem, t_high, t_low, *what)
        elif name == "I":
            xy_event(*i_all, *what)
        elif name == "A":
            xy_event(*a_all, *what)
        elif name == "own" and what[0] == "X":
            z_first()
        elif name == "own" and what[0] == "I":
            xy_own(i_ref, *i_all, what[1])
        elif name == "own":
            xy_own(a_ref, *a_all, what[1])
        elif name == "comp":
            t_event(*what)
        else:
            r_event(*what)
    part = pl.ds(pl.multiple_of((1 - c) * rows, rows), rows)
    send(total.at[part], o_ref.at[c], r_sem, sibling)
    for name, *what in ORDER:
        if name == "R":
            r_event(*what, own=0)
    o_ref[c] = total[pl.ds(pl.multiple_of(c * rows, rows), rows), :]
    arrived(o_ref.at[1 - c], r_sem)
    for copy in started:
        copy.wait_send()


def shards(amplitudes, integrals, nx, ny, nz):
    classes, rows, width = amplitudes.shape
    f32, b16 = jnp.float32, jnp.bfloat16
    dma = pltpu.SemaphoreType.DMA
    return pl.pallas_call(
        functools.partial(kernel, nx, ny, nz),
        out_shape=jax.ShapeDtypeStruct(amplitudes.shape, f32),
        in_specs=[pl.BlockSpec(memory_space=pltpu.VMEM)] * 2,
        out_specs=pl.BlockSpec(memory_space=pltpu.VMEM),
        scratch_shapes=[
            pltpu.VMEM((nz, 2, rows, width), f32),
            pltpu.VMEM((nx * ny, 2, rows, width), f32),
            pltpu.VMEM((nx * ny, 2, rows, width), f32),
            pltpu.VMEM((nz, 2, rows, width), f32),
            pltpu.VMEM((2 * rows, width), f32),
            pltpu.VMEM((nz, 2, rows, width), b16),
            pltpu.VMEM((nz, 2, rows, width), b16),
            pltpu.VMEM((nx * ny, 2, rows, width), b16),
            pltpu.VMEM((nx * ny, 2, rows, width), b16),
            pltpu.VMEM((nx * ny, 2, rows, width), b16),
            pltpu.VMEM((nx * ny, 2, rows, width), b16),
            pltpu.VMEM((nz, 2, rows, width), b16),
            pltpu.VMEM((nz, 2, rows, width), b16),
            dma((160,)),
            dma((2, nz, 2)),
            dma((2, nx * ny)),
            dma((2, nx * ny)),
            dma((2, nz, 2)),
            dma,
        ],
        compiler_params=pltpu.CompilerParams(
            collective_id=0, has_side_effects=True, vmem_limit_bytes=48 * 1024 * 1024
        ),
    )(amplitudes, integrals)


def solution(mesh):
    nz = mesh.shape["int"]
    nx = ny = 4
    placed = P(None, "pair", "int")
    return jax.shard_map(
        functools.partial(shards, nx=nx, ny=ny, nz=nz),
        mesh=mesh, in_specs=(placed, placed), out_specs=placed, check_vma=False,
    )
```
